256 devices in a mesh: delay: 8 (over y, core), row: 32 (over x, z).
Axes of the slice: x: 4, y: 4, z: 8, core: 2. Of those that a mesh axis runs over, the one named last changes fastest.
Arguments:
- incident: bfloat16 [3, 16384, 128], P(None, 'row'), may hold values from -6 to 6
- history: float32 [16, 16384, 128], P('delay', 'row'), may hold values from -6 to 6
- couplings: bfloat16 [16, 16384, 2048], P('delay', 'row'), may hold values from -0.06591797 to 0.06591797
- block_inverse: float32 [128, 128, 128], P('row')
- load_coeff: float32 [16384], P('row'), may hold values from 0.02 to 0.2
- pattern: int32 [16, 128, 16], P('delay', 'row'), may hold values from 0 to 63, as said below
- wanted: int32 [32, 32, 2], replicated, may hold values from -1 to 3, as said below
Outputs:
- currents: bfloat16 [3, 16384, 128], P(None, 'row')
- future: float32 [16, 16384, 128], P('delay', 'row')
The draws below stay inside these ranges and needn't reach their ends.
Inputs may be any that keep to these rules, and one draw needn't show every extreme that they name: wanted[q, p, c] for c below a count is a distinct local block index of row owner p that owner q needs, and -1 after it; every owner needs between 1 and 2 blocks of every owner, and exactly 2 of its own. pattern[l, i, s] over s are 16 distinct slots p * 2 + c whose entry wanted[q, p, c] is not -1, q the row owner of block row i; every such slot of q is named by some row of that owner.
All inputs are finite; a program needn't handle non-finite values.
Results may differ from the reference program's by a relative error of at most 0.009.
Values may be sent and summed in bfloat16 or wider, within the bound.
A program may use at most 64 MiB of HBM per device.

```python
import math
import jax
import jax.numpy as jnp
from jax import lax

BS = 128
ROWNZ = 16
DELAYS = 16
BLK_DEV = 4
EXC = 128
STEPS = 3
NB = 128
N = 16384
CAP = 2
N_ROW = 32


def draw_block_inverse(key, part):
    noise = jax.random.normal(jax.random.fold_in(key, 3), (NB, BS, BS), jnp.float32)
    return jnp.eye(BS, dtype=jnp.float32)[None] + noise * (0.6 / BS ** 0.5)


def routing_tables(key):
    base = jax.random.fold_in(key, 11)
    key_count, key_local, key_mix, key_offset = jax.random.split(base, 4)
    counts = jax.random.randint(key_count, (N_ROW, N_ROW), CAP // 2, CAP + 1)
    counts = jnp.where(jnp.eye(N_ROW, dtype=bool), CAP, counts)
    scores = jax.random.randint(key_local, (N_ROW, N_ROW, BLK_DEV), 0, 1 << 20) * BLK_DEV + jnp.arange(BLK_DEV)
    order = jnp.argsort(scores, axis=-1).astype(jnp.int32)
    picks = order[:, :, :CAP]
    live = jnp.arange(CAP)[None, None, :] < counts[:, :, None]
    wanted = jnp.where(live, picks, -1).astype(jnp.int32)
    width = N_ROW * CAP
    slot_ids = jnp.broadcast_to(jnp.arange(width, dtype=jnp.int32)[None, :], (N_ROW, width))
    flat_live = live.reshape(N_ROW, width)
    mixing = jax.random.randint(key_mix, (N_ROW, width), 0, 1 << 20) * width + jnp.arange(width)
    ranking = jnp.where(flat_live, mixing, (1 << 30) + jnp.arange(width))
    ranked = jnp.take_along_axis(slot_ids, jnp.argsort(ranking, axis=-1), axis=1)
    sizes_owner = jnp.sum(counts, axis=1)
    total_rows = DELAYS * BLK_DEV
    starts = jnp.arange(total_rows)[None, :] * ROWNZ
    randoms = jax.random.randint(key_offset, (N_ROW, total_rows), 0, 1 << 20) % sizes_owner[:, None]
    offsets = jnp.where(starts < sizes_owner[:, None], starts, randoms)
    picks_row = (offsets[:, :, None] + jnp.arange(ROWNZ)[None, None, :]) % sizes_owner[:, None, None]
    chosen = jnp.take_along_axis(ranked, picks_row.reshape(N_ROW, total_rows * ROWNZ), axis=1)
    chosen = chosen.reshape(N_ROW, DELAYS, BLK_DEV, ROWNZ).transpose(1, 0, 2, 3)
    return (chosen.reshape(DELAYS, N_ROW * BLK_DEV, ROWNZ).astype(jnp.int32), wanted)


def draw_pattern(key, part):
    return routing_tables(key)[0]


def draw_wanted(key, part):
    return routing_tables(key)[1]


def steps_of(own_key, dims, pieces, low, high):
    level, own = 1.0, jax.random.fold_in(own_key, 6)
    for position, shards_of in pieces:
        steps = jnp.exp(jax.random.uniform(jax.random.fold_in(own, position), (shards_of,), jnp.float32, low / len(pieces), high / len(pieces)))
        level = level * jnp.repeat(steps, dims[position] // shards_of).reshape([-1 if axis == position else 1 for axis in range(len(dims))])
    return level


def gaussian(rng, shape, deviation, reach, shards=(), kind=jnp.bfloat16):
    factor_of = steps_of(rng, shape, shards, -0.22, 0.18) if shards else 1.0
    result = jax.random.normal(rng, shape, jnp.float32) * deviation * factor_of
    return jnp.minimum(jnp.maximum(result, -reach), reach).astype(kind)


def setup_inputs(seed: int = 0) -> dict:
    splits = jax.random.split(jax.random.key(seed), 8)
    return {
        "incident": gaussian(splits[0], (STEPS, N, EXC), 1.0, 6.0, ((1, 32),)),
        "history": gaussian(splits[1], (DELAYS, N, EXC), 1.0, 6.0, ((0, 8), (1, 32)), jnp.float32),
        "couplings": gaussian(splits[2], (DELAYS, N, ROWNZ * BS), (0.5 / (ROWNZ * BS) ** 0.5), 0.06591797, ((0, 8), (1, 32))),
        "block_inverse": draw_block_inverse(jax.random.fold_in(splits[7], 71), 0),
        "load_coeff": jnp.clip(jnp.exp(math.log(0.2) - 2.3025851 * jax.random.uniform(splits[4], (N,), jnp.float32) ** steps_of(splits[4], (N,), ((0, 32),), -0.2, 0.2)), 0.02, 0.2),
        "pattern": draw_pattern(jax.random.fold_in(splits[7], 71), 0),
        "wanted": draw_wanted(jax.random.fold_in(splits[7], 71), 0),
    }


def reference(incident, history, couplings, block_inverse, load_coeff, pattern, wanted):
    nblk = N // BS
    acc = history
    zmats = couplings.reshape(DELAYS, nblk, BS, ROWNZ * BS)
    row_owner = (jnp.arange(nblk, dtype=jnp.int32) // BLK_DEV).astype(jnp.int32)
    src_owner = (pattern // CAP).astype(jnp.int32)
    src_slot = (pattern % CAP).astype(jnp.int32)
    local = wanted[row_owner[None, :, None], src_owner, src_slot]
    columns = (src_owner * BLK_DEV + jnp.maximum(local, 0)).astype(jnp.int32)
    outputs = []
    for step in range(STEPS):
        rhs = incident[step].astype(jnp.float32) - acc[0]
        solved = jnp.einsum("iab,ibc->iac", block_inverse, rhs.reshape(nblk, BS, EXC),
                            precision=lax.Precision.HIGHEST).reshape(N, EXC)
        current = (solved - load_coeff[:, None] * solved * solved * solved).astype(jnp.bfloat16)
        outputs.append(current)
        blocks = current.reshape(nblk, BS, EXC)

        def one_delay(pair):
            zmat, cols = pair
            picked = blocks[cols].reshape(nblk, ROWNZ * BS, EXC)
            return jnp.einsum("iab,ibc->iac", zmat.astype(jnp.float32), picked.astype(jnp.float32)).reshape(N, EXC)

        products = lax.map(one_delay, (zmats, columns))
        shifted = jnp.concatenate([acc[1:], jnp.zeros((1, N, EXC), jnp.float32)], 0)
        acc = shifted + products
    return jnp.stack(outputs), acc
```

```python
import jax
import jax.numpy as jnp
from jax import lax
from jax.experimental import pallas as pl
from jax.experimental.pallas import tpu as pltpu
from jax.sharding import PartitionSpec as P

STEPS = 3
NX, NY, NZ = 4, 4, 8
PIECES = 2 * NY
BLK = 4
CAP = 2
GROUP = NZ * CAP
SLOTS = NX * GROUP
PICKS = 16
TOGETHER = 4
BF16, F32 = jnp.bfloat16, jnp.float32
HIGHEST = lax.Precision.HIGHEST


def kernel(
    inc_hbm, hist_hbm, z_hbm, binv_hbm, lc_ref, pat, sel, cur_hbm, fut_hbm,
    inc, acc, zmat, binv, outv, pass_out, pass_in, cut, staged, *rest,
):
    zblk, got = rest[:STEPS], rest[STEPS : 2 * STEPS]
    (
        local_sem, out_sem, pass_ss, pass_rs, cut_ss, cut_rs, z_ss, z_rs, x_ss, x_rs,
        up_ss, up_rs, down_ss, down_rs, fwd_ss, fwd_rs, core_ss, core_rs,
    ) = rest[2 * STEPS :]
    d, q = lax.axis_index("delay"), lax.axis_index("row")
    y, k = d // 2, d % 2
    x, z = q // NZ, q % NZ
    rows = PIECES * 16
    up, down, far = (lax.rem(y + s, NY) * 2 + k for s in (1, NY - 1, 2))
    other = y * 2 + 1 - k
    sent = []

    def remote(src, dst, ss, rs, dd, qq):
        return pltpu.make_async_remote_copy(
            src_ref=src, dst_ref=dst, send_sem=ss, recv_sem=rs, device_id=(dd, qq),
            device_id_type=pl.DeviceIdType.MESH,
        )

    def send(*args):
        copy = remote(*args)
        copy.start()
        sent.append(copy)

    loads = [
        pltpu.make_async_copy(hist_hbm, acc, local_sem.at[0]),
        pltpu.make_async_copy(inc_hbm, inc, local_sem.at[1]),
        pltpu.make_async_copy(binv_hbm, binv, local_sem.at[2]),
        pltpu.make_async_copy(z_hbm, zmat, local_sem.at[3]),
    ]
    for load in loads:
        load.start()

    barrier = pltpu.get_barrier_semaphore()
    peers = [(lax.rem(d + s, PIECES), q) for s in range(1, PIECES)]
    peers += [(d, x * NZ + lax.rem(z + s, NZ)) for s in range(1, NZ)]
    peers += [(d, lax.rem(x + s, NX) * NZ + z) for s in range(1, NX)]
    for peer in peers:
        pl.semaphore_signal(barrier, inc=1, device_id=peer, device_id_type=pl.DeviceIdType.MESH)
    loads[0].wait()
    pass_out[0] = acc[0].astype(BF16)

    @pl.when(d == PIECES - 1)
    def _():
        pass_in[...] = jnp.zeros_like(pass_in)

    loads[1].wait()
    loads[2].wait()
    pl.semaphore_wait(barrier, len(peers))

    def passing(n):
        return remote(pass_out.at[n], pass_in.at[n], pass_ss.at[n], pass_rs.at[n], lax.rem(d + PIECES - 1, PIECES), q)

    def scatter(n, e):
        return remote(cut.at[n, e], zblk[n].at[z], cut_ss.at[n, e], cut_rs.at[n], e, q)

    def solve(n):
        for i in range(BLK):
            part = pl.ds(i * rows, rows)
            load = jnp.broadcast_to(lc_ref[pl.ds(i, 1), :], (rows, rows)).T
            rhs = inc[n, part, :].astype(F32) - acc[0, part, :]
            solved = jnp.dot(binv[i], rhs, precision=HIGHEST, preferred_element_type=F32)
            current = (solved - load * solved * solved * solved).astype(BF16)
            cut[n, :, i] = current.reshape(PIECES, 16, rows)

    def product(n, half, i):
        total = None
        for s in range(0, PICKS, TOGETHER):
            picked = [got[n][:, pat[(half * BLK + i) * PICKS + s + t]].reshape(rows, rows) for t in range(TOGETHER)]
            part = jnp.dot(
                zmat[half, pl.ds(pl.multiple_of(i * rows, rows), rows), pl.ds(s * rows, TOGETHER * rows)],
                jnp.concatenate(picked, axis=0),
                preferred_element_type=F32,
            )
            total = part if total is None else total + part
        return total

    def first_product(n):
        def body(i, carry):
            part = pl.ds(pl.multiple_of(i * rows, rows), rows)
            acc[0, part, :] = acc[1, part, :] + product(n, 0, i)
            return carry

        lax.fori_loop(0, BLK, body, 0)

    def second_product(n):
        @pl.when(d < PIECES - 1)
        def _():
            passing(n).wait_recv()

        def body(i, carry):
            part = pl.ds(pl.multiple_of(i * rows, rows), rows)
            acc[1, part, :] = pass_in[n, part, :].astype(F32) + product(n, 1, i)
            return carry

        lax.fori_loop(0, BLK, body, 0)
        outv[n] = got[n][:, pl.ds(SLOTS, BLK)].transpose(1, 0, 2, 3)
        pltpu.make_async_copy(outv.at[n], cur_hbm.at[n], out_sem.at[n]).start()

    for n in range(STEPS):
        zb, g = zblk[n], got[n]

        @pl.when(d == 0)
        def _():
            solve(n)
            for e in range(1, PIECES):
                scatter(n, e).start()
            zb[z] = cut[n, 0]

        @pl.when(d > 0)
        def _():
            passing(n).start()
            scatter(n, 1).wait_recv()

        for s in (4, 3, 5, 2, 6, 1, 7):
            if s < NZ:
                to = lax.rem(z + s, NZ)
                send(zb.at[z], zb.at[z], z_ss.at[n, s], z_rs.at[n, z], d, x * NZ + to)
        if n:
            second_product(n - 1)
        g[d, pl.ds(SLOTS, BLK)] = zb[z]

        chunks = [(SLOTS, BLK)] + [(lax.rem(x + s, NX) * GROUP, GROUP) for s in (0, *[t for t in (1, 3, 2) if t < NX])]
        to_up = [j for j in (1, 3) if j < len(chunks)]

        def chunk(e, j):
            return g.at[e, pl.ds(*chunks[j])]

        def spread(j):
            send(chunk(d, j), chunk(d, j), up_ss.at[n, j], up_rs.at[n, j], up, q)
            send(chunk(d, j), chunk(d, j), down_ss.at[n, j], down_rs.at[n, j], down, q)

        def forward(j):
            remote(chunk(down, j), chunk(down, j), up_ss.at[n, j], up_rs.at[n, j], down, q).wait_recv()
            remote(chunk(up, j), chunk(up, j), down_ss.at[n, j], down_rs.at[n, j], up, q).wait_recv()
            e, to = (down, up) if j in to_up else (up, down)
            send(chunk(e, j), chunk(e, j), fwd_ss.at[n, j], fwd_rs.at[n, j], to, q)

        def across(e, t):
            send(g.at[e], g.at[e], core_ss.at[n, t], core_rs.at[n, t], other, q)

        for s in range(1, NZ):
            there = lax.rem(z + s, NZ)
            remote(zb.at[there], zb.at[there], z_ss.at[n, s], z_rs.at[n, there], d, x * NZ + there).wait_recv()

        for s in (2, 1, 3, 0):
            if s < NX:
                to = lax.rem(x + s, NX)
                for t in range(GROUP):
                    piece = zb[t // CAP, sel[to * GROUP + t]]
                    if s:
                        staged[n, s - 1, t] = piece
                    else:
                        g[d, x * GROUP + t] = piece
                if s:
                    here = g.at[d, pl.ds(x * GROUP, GROUP)]
                    send(staged.at[n, s - 1], here, x_ss.at[n, s - 1], x_rs.at[n, s - 1], d, to * NZ + z)
        spread(0)
        spread(1)
        waiting = [0, 1]
        for j, s in enumerate([t for t in (1, 3, 2) if t < NX], 2):
            from_x = lax.rem(x + s, NX)
            remote(
                staged.at[n, NX - s - 1], chunk(d, j), x_ss.at[n, NX - s - 1], x_rs.at[n, NX - s - 1], d, from_x * NZ + z
            ).wait_recv()
            spread(j)
            for w in waiting:
                forward(w)
            waiting = [j]
        across(d, 0)
        for w in waiting:
            forward(w)
        across(up, 1)
        across(down, 2)
        for j in range(len(chunks)):
            frm = down if j in to_up else up
            remote(chunk(far, j), chunk(far, j), fwd_ss.at[n, j], fwd_rs.at[n, j], frm, q).wait_recv()
        across(far, 3)
        for t, s in enumerate((0, 1, NY - 1, 2)):
            e = lax.rem(y + s, NY) * 2 + 1 - k
            remote(g.at[e], g.at[e], core_ss.at[n, t], core_rs.at[n, t], other, q).wait_recv()

        if n == 0:
            loads[3].wait()
        first_product(n)
        if n < STEPS - 1:
            pass_out[n + 1] = acc[0].astype(BF16)

    pltpu.make_async_copy(acc.at[0], fut_hbm.at[0], out_sem.at[STEPS]).start()
    second_product(STEPS - 1)
    pltpu.make_async_copy(acc.at[1], fut_hbm.at[1], out_sem.at[STEPS + 1]).start()
    for copy in sent:
        copy.wait_send()

    @pl.when(d == 0)
    def _():
        for n in range(STEPS):
            for e in range(1, PIECES):
                scatter(n, e).wait_send()

    @pl.when(d > 0)
    def _():
        for n in range(STEPS):
            passing(n).wait_send()

    for n in range(STEPS):
        pltpu.make_async_copy(outv.at[n], cur_hbm.at[n], out_sem.at[n]).wait()
    for h in range(2):
        pltpu.make_async_copy(acc.at[h], fut_hbm.at[h], out_sem.at[STEPS + h]).wait()


def local(incident, history, couplings, block_inverse, load_coeff, pattern, wanted):
    size = block_inverse.shape[1]
    mine = BLK * size
    q = lax.axis_index("row")
    x, z = q // NZ, q % NZ
    table = wanted.reshape(NX, NZ, NX, NZ, CAP)
    table = lax.dynamic_slice(table, (0, z, x, 0, 0), (NX, 1, 1, NZ, CAP))
    table = jnp.maximum(table, 0).reshape(NX * GROUP)
    anywhere = pl.BlockSpec(memory_space=pl.ANY)
    dma = pltpu.SemaphoreType.DMA
    currents, future = pl.pallas_call(
        kernel,
        out_shape=(
            jax.ShapeDtypeStruct((STEPS, BLK, PIECES, 16, size), BF16),
            jax.ShapeDtypeStruct((2, mine, size), F32),
        ),
        in_specs=[anywhere] * 4
        + [pl.BlockSpec(memory_space=pltpu.VMEM), pl.BlockSpec(memory_space=pltpu.SMEM), pl.BlockSpec(memory_space=pltpu.SMEM)],
        out_specs=(anywhere, anywhere),
        scratch_shapes=[
            pltpu.VMEM((STEPS, mine, size), BF16),
            pltpu.VMEM((2, mine, size), F32),
            pltpu.VMEM((2, mine, PICKS * size), BF16),
            pltpu.VMEM((BLK, size, size), F32),
            pltpu.VMEM((STEPS, BLK, PIECES, 16, size), BF16),
            pltpu.VMEM((STEPS, mine, size), BF16),
            pltpu.VMEM((STEPS, mine, size), BF16),
            pltpu.VMEM((STEPS, PIECES, BLK, 16, size), BF16),
            pltpu.VMEM((STEPS, NX - 1, GROUP, 16, size), BF16),
            *[pltpu.VMEM((NZ, BLK, 16, size), BF16) for _ in range(STEPS)],
            *[pltpu.VMEM((PIECES, SLOTS + BLK, 16, size), BF16) for _ in range(STEPS)],
            dma((4,)),
            dma((STEPS + 2,)),
            dma((STEPS,)), dma((STEPS,)),
            dma((STEPS, PIECES)), dma((STEPS,)),
            dma((STEPS, NZ)), dma((STEPS, NZ)),
            dma((STEPS, NX - 1)), dma((STEPS, NX - 1)),
            dma((STEPS, NX + 1)), dma((STEPS, NX + 1)),
            dma((STEPS, NX + 1)), dma((STEPS, NX + 1)),
            dma((STEPS, NX + 1)), dma((STEPS, NX + 1)),
            dma((STEPS, 4)), dma((STEPS, 4)),
        ],
        compiler_params=pltpu.CompilerParams(
            collective_id=0, has_side_effects=True, vmem_limit_bytes=40 * 2**20
        ),
        name="march",
    )(
        incident, history, couplings, block_inverse, load_coeff.reshape(BLK, size),
        pattern.reshape(-1), table,
    )
    return currents.reshape(STEPS, mine, size), future


def solution(mesh):
    in_specs = (
        P(None, "row", None),
        P("delay", "row", None),
        P("delay", "row", None),
        P("row", None, None),
        P("row"),
        P("delay", "row", None),
        P(),
    )
    out_specs = (P(None, "row", None), P("delay", "row", None))
    return jax.shard_map(local, mesh=mesh, in_specs=in_specs, out_specs=out_specs, check_vma=False)
```

```python
import jax
import jax.numpy as jnp
from jax import lax
from jax.experimental import pallas as pl
from jax.experimental.pallas import tpu as pltpu
from jax.sharding import PartitionSpec as P

STEPS = 3
NX, NY, NZ = 4, 4, 8
PIECES = 2 * NY
BLK = 4
CAP = 2
GROUP = NZ * CAP
SLOTS = NX * GROUP
PICKS = 16
HELD = 3
TOGETHER = 4
BF16, F32 = jnp.bfloat16, jnp.float32
HIGHEST = lax.Precision.HIGHEST


def kernel(
    inc_hbm, hist_hbm, z_hbm, binv_hbm, pat_hbm, lc_ref, pat, wanted, cur_ref, fut_ref,
    inc, acc, zmat, binv, pass_out, pass_in, staged, cut, slices, share_z, pat_in, pat0, base, share, share_out, share_in, *rest,
):
    zblk, own, got = rest[:STEPS], rest[STEPS : 2 * STEPS], rest[2 * STEPS : 3 * STEPS]
    (
        local_sem, pass_ss, pass_rs, cut_ss, cut_rs, z_ss, z_rs, x_ss, x_rs, up_ss, up_rs, down_ss, down_rs,
        fwd_ss, fwd_rs, core_ss, core_rs, slice_ss, slice_rs, pat_ss, pat_rs, base_ss, base_rs, share_ss, share_rs,
    ) = rest[3 * STEPS :]
    d, q = lax.axis_index("delay"), lax.axis_index("row")
    y, k = d // 2, d % 2
    x, z = q // NZ, q % NZ
    rows = PIECES * 16
    up, down, far = (lax.rem(y + s, NY) * 2 + k for s in (1, NY - 1, 2))
    other = y * 2 + 1 - k
    sent = []

    def remote(src, dst, ss, rs, dd, qq):
        return pltpu.make_async_remote_copy(
            src_ref=src, dst_ref=dst, send_sem=ss, recv_sem=rs, device_id=(dd, qq),
            device_id_type=pl.DeviceIdType.MESH,
        )

    def send(*args):
        copy = remote(*args)
        copy.start()
        sent.append((copy, None))

    def send_if(cond, *args):
        copy = remote(*args)
        pl.when(cond)(copy.start)
        sent.append((copy, cond))

    loads = [
        pltpu.make_async_copy(hist_hbm, acc, local_sem.at[0]),
        pltpu.make_async_copy(inc_hbm, inc, local_sem.at[1]),
        pltpu.make_async_copy(binv_hbm, binv, local_sem.at[2]),
        pltpu.make_async_copy(z_hbm, zmat, local_sem.at[3]),
    ]
    for load in loads:
        load.start()

    barrier = pltpu.get_barrier_semaphore()
    peers = [(lax.rem(d + s, PIECES), q) for s in range(1, PIECES)]
    peers += [(d, x * NZ + lax.rem(z + s, NZ)) for s in range(1, NZ)]
    peers += [(d, lax.rem(x + s, NX) * NZ + z) for s in range(1, NX)]
    for peer in peers:
        pl.semaphore_signal(barrier, inc=1, device_id=peer, device_id_type=pl.DeviceIdType.MESH)

    def finish(b, rhs):
        load = jnp.broadcast_to(lc_ref[pl.ds(b, 1), :], (rows, rows)).T
        solved = jnp.dot(binv[b], rhs, precision=HIGHEST, preferred_element_type=F32)
        return (solved - load * solved * solved * solved).astype(BF16).reshape(PIECES, 16, rows)

    def part_of(b):
        return pl.ds(b * rows if isinstance(b, int) else pl.multiple_of(b * rows, rows), rows)

    def slice_z():
        def body(i, carry):
            for s in range(PICKS):
                tile = zmat[0, part_of(i), pl.ds(s * rows, rows)]
                slices[:, i, s] = tile.T.reshape(PIECES, 16, rows)
            return carry

        lax.fori_loop(0, BLK, body, 0)

    for load in loads[:3]:
        load.wait()

    @pl.when(d == 0)
    def _():
        for i in range(BLK):
            cut[0, :, i] = finish(i, inc[0, part_of(i), :].astype(F32) - acc[0, part_of(i), :])
        loads[3].wait()
        slice_z()
        share_z[...] = slices[0]
        base[0] = acc[1, part_of(0), :]

    @pl.when(d > 0)
    def _():
        loads[3].wait()

    pass_out[0] = acc[0].astype(BF16)

    @pl.when(d == PIECES - 1)
    def _():
        pass_in[...] = jnp.zeros_like(pass_in)

    pl.semaphore_wait(barrier, len(peers))

    def passing(n):
        return remote(pass_out.at[n], pass_in.at[n], pass_ss.at[n], pass_rs.at[n], lax.rem(d + PIECES - 1, PIECES), q)

    def pass_on(n):
        pl.when(d > 0)(passing(n).start)
        sent.append((passing(n), d > 0))

    def product(n, half, i):
        total = None
        for s in range(0, PICKS, TOGETHER):
            picked = [got[n][:, pat[half, i, s + t]].reshape(rows, rows) for t in range(TOGETHER)]
            part = jnp.dot(
                zmat[half, part_of(i), pl.ds(s * rows, TOGETHER * rows)],
                jnp.concatenate(picked, axis=0),
                preferred_element_type=F32,
            )
            total = part if total is None else total + part
        return total

    def first_product(n, out):
        def body(i, carry):
            out[0, part_of(i), :] = acc[1, part_of(i), :] + product(n, 0, i)
            return carry

        lax.fori_loop(0, BLK, body, 0)

    def second_product(n, out):
        @pl.when(d < PIECES - 1)
        def _():
            passing(n).wait_recv()

        def body(i, carry):
            out[1, part_of(i), :] = pass_in[n, part_of(i), :].astype(F32) + product(n, 1, i)
            return carry

        lax.fori_loop(0, BLK, body, 0)
        cur_ref[n] = got[n][:, pl.ds(SLOTS, BLK)].transpose(1, 0, 2, 3)

    def products(n):
        @pl.when(d > 0)
        def _():
            first_product(n, acc)
            pass_out[n + 1] = acc[0].astype(BF16)

        pass_on(n + 1)
        if n == 1:
            @pl.when(d == 0)
            def _():
                for b in range(1, BLK):
                    remote(*base_args(1, b)).wait_send()

        second_product(n, acc)
        if n == 0:
            @pl.when(d == 0)
            def _():
                for b in range(1, BLK):
                    remote(*base_args(1, b)).start()
                base[1] = acc[1, part_of(0), :]

    def base_args(m, b):
        src = hist_hbm.at[1, part_of(b)] if m == 0 else acc.at[1, part_of(b)]
        return src, base.at[m], base_ss.at[m, b], base_rs.at[m], 2 * b, q

    xs = [s for s in (1, 3, 2) if s < NX]
    chunks = [(SLOTS, BLK)] + [(lax.rem(x + s, NX) * GROUP, GROUP) for s in (0, *xs)]
    to_up = [j for j in (1, 3) if j < len(chunks)]

    def chunk(n, e, j):
        return got[n].at[e, pl.ds(*chunks[j])]

    def spread(n, j):
        src = own[n].at[pl.ds(*chunks[j])]
        send(src, chunk(n, d, j), up_ss.at[n, j], up_rs.at[n, j], up, q)
        send(src, chunk(n, d, j), down_ss.at[n, j], down_rs.at[n, j], down, q)

    def forward(n, j):
        remote(chunk(n, down, j), chunk(n, down, j), up_ss.at[n, j], up_rs.at[n, j], down, q).wait_recv()
        remote(chunk(n, up, j), chunk(n, up, j), down_ss.at[n, j], down_rs.at[n, j], up, q).wait_recv()
        e, to = (down, up) if j in to_up else (up, down)
        send(chunk(n, e, j), chunk(n, e, j), fwd_ss.at[n, j], fwd_rs.at[n, j], to, q)

    def across(n, e, t):
        src = own[n] if t == 0 else got[n].at[e]
        send(src, got[n].at[e], core_ss.at[n, t], core_rs.at[n, t], other, q)

    def forwards(n, js):
        for j in js:
            forward(n, j)

    def last_hops(n):
        for j in range(len(chunks)):
            frm = down if j in to_up else up
            remote(chunk(n, far, j), chunk(n, far, j), fwd_ss.at[n, j], fwd_rs.at[n, j], frm, q).wait_recv()
        across(n, far, 3)

    def gathered(n):
        for t, s in enumerate((0, 1, NY - 1, 2)):
            e = lax.rem(y + s, NY) * 2 + 1 - k
            remote(got[n].at[e], got[n].at[e], core_ss.at[n, t], core_rs.at[n, t], other, q).wait_recv()

    for n in range(STEPS):
        zb = zblk[n]
        if n == 0:
            for e in range(1, PIECES):
                send_if(d == 0, cut.at[0, e], zb.at[z], cut_ss.at[0, e], cut_rs.at[0, 0], e, q)

            @pl.when(d == 0)
            def _():
                zb[z] = cut[0, 0]

            @pl.when(d > 0)
            def _():
                remote(cut.at[0, 1], zb.at[z], cut_ss.at[0, 1], cut_rs.at[0, 0], 0, q).wait_recv()

        else:
            m = n - 1

            @pl.when(k == 0)
            def _():
                @pl.when(d > 0)
                def _():
                    remote(base.at[m], base.at[m], base_ss.at[m, 1], base_rs.at[m], 0, q).wait_recv()

                rhs = inc[n, part_of(y), :].astype(F32) - base[m] - share[y]
                for s in range(1, PIECES):
                    e = lax.rem(d + s, PIECES)
                    here = share_in.at[m, e]
                    remote(here, here, share_ss.at[m, 0], share_rs.at[m, e], e, q).wait_recv()
                    rhs = rhs - share_in[m, e].astype(F32)
                cut[n, :, 0] = finish(y, rhs)

            for s in range(1, PIECES):
                e = lax.rem(d + s, PIECES)
                send_if(k == 0, cut.at[n, e, 0], zb.at[z, y], cut_ss.at[n, s], cut_rs.at[n, y], e, q)

            @pl.when(k == 0)
            def _():
                zb[z, y] = cut[n, d, 0]

            for b in range(BLK):
                @pl.when(d != 2 * b)
                def _():
                    remote(zb.at[z, b], zb.at[z, b], cut_ss.at[n, 1], cut_rs.at[n, b], 2 * b, q).wait_recv()

        for s in (4, 3, 5, 2, 6, 1, 7):
            if s < NZ:
                to = lax.rem(z + s, NZ)
                send(zb.at[z], zb.at[z], z_ss.at[n, s], z_rs.at[n, z], d, x * NZ + to)
        own[n][pl.ds(SLOTS, BLK)] = zb[z]
        if n == 0:
            for e in range(1, PIECES):
                send_if(d == 0, pat_hbm, pat_in, pat_ss.at[e], pat_rs.at[0], e, q)
            for e in (4, 5, 2, 3, 6, 7, 1):
                send_if(d == 0, slices.at[e], share_z, slice_ss.at[e], slice_rs.at[0], e, q)
            for b in range(1, BLK):
                send_if(d == 0, *base_args(0, b))
            pass_on(0)
        else:
            for j in range(HELD, len(chunks)):
                spread(n - 1, j)

        for s in range(1, NZ):
            there = lax.rem(z + s, NZ)
            remote(zb.at[there], zb.at[there], z_ss.at[n, s], z_rs.at[n, there], d, x * NZ + there).wait_recv()

        for s in (2, 1, 3, 0):
            if s < NX:
                to = lax.rem(x + s, NX)
                for t in range(GROUP):
                    piece = zb[t // CAP, jnp.maximum(wanted[to * NZ + z, t % CAP, x * NZ + t // CAP], 0)]
                    if s:
                        staged[n, s - 1, t] = piece
                    else:
                        own[n][x * GROUP + t] = piece
                if s:
                    here = own[n].at[pl.ds(x * GROUP, GROUP)]
                    send(staged.at[n, s - 1], here, x_ss.at[n, s - 1], x_rs.at[n, s - 1], d, to * NZ + z)

        if n == 0:
            @pl.when(d > 0)
            def _():
                remote(pat_hbm, pat_in, pat_ss.at[1], pat_rs.at[0], 0, q).wait_recv()

            @pl.when(d == 0)
            def _():
                copy = pltpu.make_async_copy(pat_hbm, pat_in, local_sem.at[4])
                copy.start()
                copy.wait()

            copy = pltpu.make_async_copy(pat_in, pat0, local_sem.at[5])
            copy.start()
            copy.wait()
        else:
            forwards(n - 1, range(len(chunks)))
            across(n - 1, up, 1)
            across(n - 1, down, 2)
            last_hops(n - 1)
        if n == STEPS - 1:
            spread(n, 0)
            spread(n, 1)

        for j, s in enumerate(xs, 2):
            from_x = lax.rem(x + s, NX)
            there = own[n].at[pl.ds(*chunks[j])]
            back = NX - s - 1
            remote(staged.at[n, back], there, x_ss.at[n, back], x_rs.at[n, back], d, from_x * NZ + z).wait_recv()
            if n == STEPS - 1:
                spread(n, j)
        if n == STEPS - 1:
            across(n, d, 0)
        got[n][d] = own[n][...]

        if n < STEPS - 1:
            if n == 0:
                @pl.when(d > 0)
                def _():
                    remote(share_z, share_z, slice_ss.at[1], slice_rs.at[0], 0, q).wait_recv()

            def body(i, carry):
                picked = jnp.concatenate([own[n][pat0[0, i, s]] for s in range(PICKS)], axis=0)
                total = lax.dot_general(
                    share_z[i].reshape(PICKS * 16, rows), picked, (((0,), (0,)), ((), ())), preferred_element_type=F32
                )
                share[i] = total
                share_out[n, i] = total.astype(BF16)
                return carry

            lax.fori_loop(0, BLK, body, 0)
            for b in range(BLK):
                send_if(d != 2 * b, share_out.at[n, b], share_in.at[n, d], share_ss.at[n, b], share_rs.at[n, d], 2 * b, q)
            for j in range(HELD):
                spread(n, j)
            across(n, d, 0)
        if n:
            gathered(n - 1)
            products(n - 1)

    n = STEPS - 1
    forwards(n, range(len(chunks)))
    across(n, up, 1)
    across(n, down, 2)
    last_hops(n)
    gathered(n)
    first_product(n, fut_ref)
    second_product(n, fut_ref)
    for copy, cond in sent:
        if cond is None:
            copy.wait_send()
        else:
            pl.when(cond)(copy.wait_send)


def local(incident, history, couplings, block_inverse, load_coeff, pattern, wanted):
    size = block_inverse.shape[1]
    mine = BLK * size
    anywhere = pl.BlockSpec(memory_space=pl.ANY)
    numbers = pl.BlockSpec(memory_space=pltpu.SMEM)
    dma = pltpu.SemaphoreType.DMA
    chunk_sems = [dma((STEPS, NX + 1)) for _ in range(6)]
    currents, future = pl.pallas_call(
        kernel,
        out_shape=(
            pltpu.VMEM((STEPS, BLK, PIECES, 16, size), BF16),
            pltpu.VMEM((2, mine, size), F32),
        ),
        in_specs=[anywhere] * 5 + [pl.BlockSpec(memory_space=pltpu.VMEM), numbers, numbers],
        out_specs=(pl.BlockSpec(memory_space=pltpu.VMEM), pl.BlockSpec(memory_space=pltpu.VMEM)),
        scratch_shapes=[
            pltpu.VMEM((STEPS, mine, size), BF16),
            pltpu.VMEM((2, mine, size), F32),
            pltpu.VMEM((2, mine, PICKS * size), BF16),
            pltpu.VMEM((BLK, size, size), F32),
            pltpu.VMEM((STEPS, mine, size), BF16),
            pltpu.VMEM((STEPS, mine, size), BF16),
            pltpu.VMEM((STEPS, NX - 1, GROUP, 16, size), BF16),
            pltpu.VMEM((STEPS, PIECES, BLK, 16, size), BF16),
            pltpu.VMEM((PIECES, BLK, PICKS, 16, size), BF16),
            pltpu.VMEM((BLK, PICKS, 16, size), BF16),
            pltpu.VMEM(pattern.shape, jnp.int32),
            pltpu.SMEM(pattern.shape, jnp.int32),
            pltpu.VMEM((STEPS - 1, size, size), F32),
            pltpu.VMEM((BLK, size, size), F32),
            pltpu.VMEM((STEPS - 1, BLK, size, size), BF16),
            pltpu.VMEM((STEPS - 1, PIECES, size, size), BF16),
            *[pltpu.VMEM((NZ, BLK, 16, size), BF16) for _ in range(STEPS)],
            *[pltpu.VMEM((SLOTS + BLK, 16, size), BF16) for _ in range(STEPS)],
            *[pltpu.VMEM((PIECES, SLOTS + BLK, 16, size), BF16) for _ in range(STEPS)],
            dma((6,)),
            dma((STEPS,)), dma((STEPS,)),
            dma((STEPS, PIECES)), dma((STEPS, BLK)),
            dma((STEPS, NZ)), dma((STEPS, NZ)),
            dma((STEPS, NX - 1)), dma((STEPS, NX - 1)),
            *chunk_sems,
            dma((STEPS, 4)), dma((STEPS, 4)),
            dma((PIECES,)), dma((1,)),
            dma((PIECES,)), dma((1,)),
            dma((STEPS - 1, BLK)), dma((STEPS - 1,)),
            dma((STEPS - 1, BLK)), dma((STEPS - 1, PIECES)),
        ],
        compiler_params=pltpu.CompilerParams(
            collective_id=0, has_side_effects=True, vmem_limit_bytes=60 * 2**20
        ),
        name="march",
    )(
        incident, history, couplings, block_inverse, pattern, load_coeff.reshape(BLK, size),
        pattern, wanted.transpose(0, 2, 1),
    )
    return currents.reshape(STEPS, mine, size), future


def solution(mesh):
    in_specs = (
        P(None, "row", None),
        P("delay", "row", None),
        P("delay", "row", None),
        P("row", None, None),
        P("row"),
        P("delay", "row", None),
        P(),
    )
    out_specs = (P(None, "row", None), P("delay", "row", None))
    return jax.shard_map(local, mesh=mesh, in_specs=in_specs, out_specs=out_specs, check_vma=False)
```

```python
import jax
import jax.numpy as jnp
from jax import lax
from jax.experimental import pallas as pl
from jax.experimental.pallas import tpu as pltpu
from jax.sharding import PartitionSpec as P

STEPS = 3
NX, NY, NZ = 4, 4, 8
OWNERS = NX * NZ
PIECES = 2 * NY
BLK = 4
CAP = 2
GROUP = NZ * CAP
SLOTS = NX * GROUP
PICKS = 16
TOGETHER = 4
EARLY = (1, 2, 6)
BF16, F32 = jnp.bfloat16, jnp.float32
HIGHEST = lax.Precision.HIGHEST


def kernel(
    inc_hbm, hist_hbm, z_hbm, binv_hbm, pat_hbm, lc_ref, pat, wanted, cur_ref, fut_ref,
    inc, acc, zmat, binv, load, pass_out, pass_in, staged, cut, slices, share_z, pat_in, pat0,
    base_out, base, share, share_out, share_in, *rest,
):
    mine, own, got = rest[:STEPS], rest[STEPS : 2 * STEPS], rest[2 * STEPS : 3 * STEPS]
    (
        local_sem, pass_ss, pass_rs, cut_ss, cut_rs, plane_ss, plane_rs, y_ss, y_rs, core_ss, core_rs,
        slice_ss, slice_rs, pat_ss, pat_rs, base_ss, base_rs, share_ss, share_rs,
    ) = rest[3 * STEPS :]
    d, q = lax.axis_index("delay"), lax.axis_index("row")
    y, k = d // 2, d % 2
    x, z = q // NZ, q % NZ
    rows = PIECES * 16
    other = y * 2 + 1 - k
    sent = []

    def remote(src, dst, ss, rs, dd, qq):
        return pltpu.make_async_remote_copy(
            src_ref=src, dst_ref=dst, send_sem=ss, recv_sem=rs, device_id=(dd, qq),
            device_id_type=pl.DeviceIdType.MESH,
        )

    def send(*args):
        copy = remote(*args)
        copy.start()
        sent.append((copy, None))

    def send_if(cond, *args):
        copy = remote(*args)
        pl.when(cond)(copy.start)
        sent.append((copy, cond))

    def arrived(dst, rs):
        remote(dst, dst, rs, rs, other, q).wait_recv()

    def left(src, ss):
        remote(src, src, ss, ss, other, q).wait_send()

    loads = [
        pltpu.make_async_copy(hist_hbm, acc, local_sem.at[0]),
        pltpu.make_async_copy(inc_hbm, inc, local_sem.at[1]),
        pltpu.make_async_copy(binv_hbm, binv, local_sem.at[2]),
        pltpu.make_async_copy(z_hbm, zmat, local_sem.at[3]),
    ]
    for start in loads:
        start.start()

    around = [lax.rem(d + s, PIECES) for s in range(1, PIECES)]
    plane = [
        lax.rem(x + a, NX) * NZ + lax.rem(z + s, NZ) for a in (0, 1, 3, 2) for s in (4, 3, 5, 2, 6, 1, 7, 0) if a or s
    ]
    barrier = pltpu.get_barrier_semaphore()
    peers = [(e, q) for e in around] + [(d, p) for p in plane]
    for peer in peers:
        pl.semaphore_signal(barrier, inc=1, device_id=peer, device_id_type=pl.DeviceIdType.MESH)

    def part_of(b):
        return pl.ds(b * rows if isinstance(b, int) else pl.multiple_of(b * rows, rows), rows)

    def invert(b, rhs):
        solved = jnp.dot(binv[b], rhs, precision=HIGHEST, preferred_element_type=F32)
        return solved.reshape(PIECES, 16, rows)

    def loaded(solved, coefficient):
        return (solved - coefficient * solved * solved * solved).astype(BF16)

    def slice_z(half):
        def body(i, carry):
            for s in range(PICKS):
                tile = zmat[half, part_of(i), pl.ds(s * rows, rows)]
                slices[half, :, i, s] = tile.T.reshape(PIECES, 16, rows)
            return carry

        lax.fori_loop(0, BLK, body, 0)

    for start in loads[:3]:
        start.wait()
    for i in range(BLK):
        load[i] = jnp.broadcast_to(lc_ref[pl.ds(i, 1), :], (rows, rows)).T.reshape(PIECES, 16, rows)

    @pl.when(d == 0)
    def _():
        for i in range(BLK):
            cut[:, i] = loaded(invert(i, inc[0, part_of(i), :].astype(F32) - acc[0, part_of(i), :]), load[i])
        mine[0][...] = cut[0]

    loads[3].wait()

    @pl.when(d == 0)
    def _():
        slice_z(0)
        share_z[0] = slices[0, 0]

    @pl.when(d < 2)
    def _():
        for i in range(BLK):
            base_out[:, i] = invert(i, inc[1 + d, part_of(i), :].astype(F32) - acc[1 - d, part_of(i), :])
        base[d] = base_out[d]

    pass_out[0] = acc[0].astype(BF16)

    @pl.when(d == PIECES - 1)
    def _():
        pass_in[...] = jnp.zeros_like(pass_in)

    pl.semaphore_wait(barrier, len(peers))

    def passing(n):
        return remote(pass_out.at[n], pass_in.at[n], pass_ss.at[n], pass_rs.at[n], lax.rem(d + PIECES - 1, PIECES), q)

    def pass_on(n):
        pl.when(d > 0)(passing(n).start)
        sent.append((passing(n), d > 0))

    def send_slices(half, which):
        for e in which:
            send_if(d == 0, slices.at[half, e], share_z.at[half], slice_ss.at[half, e], slice_rs.at[half], e, q)

    def product(n, half, i):
        total = None
        for s in range(0, PICKS, TOGETHER):
            picked = [got[n][:, pat[half, i, s + t]].reshape(rows, rows) for t in range(TOGETHER)]
            part = jnp.dot(
                zmat[half, part_of(i), pl.ds(s * rows, TOGETHER * rows)],
                jnp.concatenate(picked, axis=0),
                preferred_element_type=F32,
            )
            total = part if total is None else total + part
        return total

    def products(n, out):
        def first(i, carry):
            out[0, part_of(i), :] = acc[1, part_of(i), :] + product(n, 0, i)
            return carry

        lax.fori_loop(0, BLK, first, 0)
        if n < STEPS - 1:
            pass_out[n + 1] = out[0].astype(BF16)
            pass_on(n + 1)

        @pl.when(d < PIECES - 1)
        def _():
            arrived(pass_in.at[n], pass_rs.at[n])

        def second(i, carry):
            out[1, part_of(i), :] = pass_in[n, part_of(i), :].astype(F32) + product(n, 1, i)
            return carry

        lax.fori_loop(0, BLK, second, 0)
        cur_ref[n] = got[n][:, pl.ds(SLOTS, BLK)].transpose(1, 0, 2, 3)

    chunks = [(SLOTS, BLK)] + [(lax.rem(x + a, NX) * GROUP, GROUP) for a in (0, 3, 1, 2)]

    def spread(n, j):
        here = pl.ds(*chunks[j])
        for t, s in enumerate((2, 1, 3)):
            remote(
                own[n].at[here], got[n].at[d, here], y_ss.at[n, t], y_rs.at[n, t], lax.rem(y + s, NY) * 2 + k, q
            ).start()

    def across(n, e, t):
        src = own[n] if t == 3 else got[n].at[e]
        send(src, got[n].at[e], core_ss.at[n, t], core_rs.at[n, t], other, q)

    def hand_over(n):
        for t, s in enumerate((2, 1, 3)):
            e = lax.rem(y + NY - s, NY) * 2 + k
            arrived(got[n].at[e], y_rs.at[n, t])
            across(n, e, t)

    def gathered(n):
        for t, s in enumerate((2, 1, 3, 0)):
            arrived(got[n].at[lax.rem(y + NY - s, NY) * 2 + 1 - k], core_rs.at[n, t])

    for n in range(STEPS):
        if n == 0:
            for e in range(1, PIECES):
                send_if(d == 0, cut.at[e], mine[0], cut_ss.at[e], cut_rs.at[0], e, q)
            for e in range(1, PIECES):
                send_if(d == 0, pat_hbm, pat_in, pat_ss.at[e], pat_rs.at[0], e, q)
            send_slices(0, (4, 5, 2, 3, 6, 7, 1))

            @pl.when(d > 0)
            def _():
                arrived(mine[0], cut_rs.at[0])

        else:
            m = n - 1

            @pl.when(d != m)
            def _():
                arrived(base.at[m], base_rs.at[m])

            arrived(share_in.at[m, pl.ds(0, PIECES - 1)], share_rs.at[m])
            for i in range(BLK):
                solved = base[m, i] - share[i, d]
                for e in around:
                    solved = solved - share_in[m, e, i].astype(F32)
                mine[n][i] = loaded(solved, load[i, d])

        for t, p in enumerate(plane):
            for c in range(CAP):
                staged[n, t, c] = mine[n][jnp.maximum(wanted[p, c, q], 0)]
            remote(staged.at[n, t], own[n].at[pl.ds(q * CAP, CAP)], plane_ss.at[n], plane_rs.at[n, x], d, p).start()
        for c in range(CAP):
            own[n][q * CAP + c] = mine[n][jnp.maximum(wanted[q, c, q], 0)]
        own[n][pl.ds(SLOTS, BLK)] = mine[n][...]

        if n == 0:
            for m in range(2):
                for s, e in enumerate(around):
                    send_if(d == m, base_out.at[e], base.at[m], base_ss.at[m, s], base_rs.at[m], e, q)
            pass_on(0)

            @pl.when(d == 0)
            def _():
                slice_z(1)
                share_z[1] = slices[1, 0]

            send_slices(1, EARLY)

            @pl.when(d > 0)
            def _():
                arrived(pat_in, pat_rs.at[0])

            @pl.when(d == 0)
            def _():
                copy = pltpu.make_async_copy(pat_hbm, pat_in, local_sem.at[4])
                copy.start()
                copy.wait()

            copy = pltpu.make_async_copy(pat_in, pat0, local_sem.at[5])
            copy.start()
            copy.wait()
        if n == STEPS - 1:
            gathered(n - 2)
            products(n - 2, acc)
            spread(n, 0)

        for j, a in enumerate((0, 3, 1, 2), 1):
            from_x = lax.rem(x + a, NX)
            there = pl.ds(0, GROUP - CAP) if a == 0 else pl.ds(*chunks[j])
            arrived(own[n].at[there], plane_rs.at[n, from_x])
            if n == STEPS - 1:
                spread(n, j)
        got[n][d] = own[n][...]

        if n < STEPS - 1:
            @pl.when(d > 0)
            def _():
                arrived(share_z.at[n], slice_rs.at[n])

            def body(i, carry):
                total = None
                for half in range(n + 1):
                    picked = jnp.concatenate([own[n - half][pat0[half, i, s]] for s in range(PICKS)], axis=0)
                    part = lax.dot_general(
                        share_z[half, i].reshape(PICKS * 16, rows), picked, (((0,), (0,)), ((), ())),
                        preferred_element_type=F32,
                    )
                    total = part if total is None else total + part
                solved = invert(i, total)
                share[i] = solved
                share_out[n, :, i] = solved.astype(BF16)
                return carry

            lax.fori_loop(0, BLK, body, 0)
            for s, e in enumerate(around):
                send(share_out.at[n, e], share_in.at[n, d], share_ss.at[n, s], share_rs.at[n], e, q)
            if n == 0:
                send_slices(1, [e for e in (4, 5, 3, 7) if e not in EARLY])
            for j in range(len(chunks)):
                spread(n, j)
        across(n, d, 3)
        if n:
            hand_over(n - 1)

    gathered(n - 1)
    products(n - 1, acc)
    hand_over(n)
    gathered(n)
    products(n, fut_ref)
    for n in range(STEPS):
        left(staged.at[n], plane_ss.at[n])
        for t in range(NY - 1):
            left(own[n], y_ss.at[n, t])
    for copy, cond in sent:
        if cond is None:
            copy.wait_send()
        else:
            pl.when(cond)(copy.wait_send)


def local(incident, history, couplings, block_inverse, load_coeff, pattern, wanted):
    size = block_inverse.shape[1]
    rows = BLK * size
    anywhere = pl.BlockSpec(memory_space=pl.ANY)
    numbers = pl.BlockSpec(memory_space=pltpu.SMEM)
    vmem = pl.BlockSpec(memory_space=pltpu.VMEM)
    dma = pltpu.SemaphoreType.DMA
    currents, future = pl.pallas_call(
        kernel,
        out_shape=(
            pltpu.VMEM((STEPS, BLK, PIECES, 16, size), BF16),
            pltpu.VMEM((2, rows, size), F32),
        ),
        in_specs=[anywhere] * 5 + [vmem, numbers, numbers],
        out_specs=(vmem, vmem),
        scratch_shapes=[
            pltpu.VMEM((STEPS, rows, size), BF16),
            pltpu.VMEM((2, rows, size), F32),
            pltpu.VMEM((2, rows, PICKS * size), BF16),
            pltpu.VMEM((BLK, size, size), F32),
            pltpu.VMEM((BLK, PIECES, 16, size), F32),
            pltpu.VMEM((STEPS, rows, size), BF16),
            pltpu.VMEM((STEPS, rows, size), BF16),
            pltpu.VMEM((STEPS, OWNERS - 1, CAP, 16, size), BF16),
            pltpu.VMEM((PIECES, BLK, 16, size), BF16),
            pltpu.VMEM((2, PIECES, BLK, PICKS, 16, size), BF16),
            pltpu.VMEM((2, BLK, PICKS, 16, size), BF16),
            pltpu.VMEM(pattern.shape, jnp.int32),
            pltpu.SMEM(pattern.shape, jnp.int32),
            pltpu.VMEM((PIECES, BLK, 16, size), F32),
            pltpu.VMEM((STEPS - 1, BLK, 16, size), F32),
            pltpu.VMEM((BLK, PIECES, 16, size), F32),
            pltpu.VMEM((STEPS - 1, PIECES, BLK, 16, size), BF16),
            pltpu.VMEM((STEPS - 1, PIECES, BLK, 16, size), BF16),
            *[pltpu.VMEM((BLK, 16, size), BF16) for _ in range(STEPS)],
            *[pltpu.VMEM((SLOTS + BLK, 16, size), BF16) for _ in range(STEPS)],
            *[pltpu.VMEM((PIECES, SLOTS + BLK, 16, size), BF16) for _ in range(STEPS)],
            dma((6,)),
            dma((STEPS,)), dma((STEPS,)),
            dma((PIECES,)), dma((1,)),
            dma((STEPS,)), dma((STEPS, NX)),
            dma((STEPS, NY - 1)), dma((STEPS, NY - 1)),
            dma((STEPS, NY)), dma((STEPS, NY)),
            dma((2, PIECES)), dma((2,)),
            dma((PIECES,)), dma((1,)),
            dma((2, PIECES)), dma((2,)),
            dma((STEPS - 1, PIECES)), dma((STEPS - 1,)),
        ],
        compiler_params=pltpu.CompilerParams(
            collective_id=0, has_side_effects=True, vmem_limit_bytes=60 * 2**20
        ),
        name="march",
    )(
        incident, history, couplings, block_inverse, pattern, load_coeff.reshape(BLK, size),
        pattern, wanted.transpose(0, 2, 1),
    )
    return currents.reshape(STEPS, rows, size), future


def solution(mesh):
    in_specs = (
        P(None, "row", None),
        P("delay", "row", None),
        P("delay", "row", None),
        P("row", None, None),
        P("row"),
        P("delay", "row", None),
        P(),
    )
    out_specs = (P(None, "row", None), P("delay", "row", None))
    return jax.shard_map(local, mesh=mesh, in_specs=in_specs, out_specs=out_specs, check_vma=False)
```

```python
import jax
import jax.numpy as jnp
from jax import lax
from jax.experimental import pallas as pl
from jax.experimental.pallas import tpu as pltpu
from jax.sharding import PartitionSpec as P

STEPS = 3
NX, NY, NZ = 4, 4, 8
OWNERS = NX * NZ
PIECES = 2 * NY
BLK = 4
CAP = 2
GROUP = NZ * CAP
SLOTS = NX * GROUP
PICKS = 16
TOGETHER = 16
EARLY = (1, 2, 6)
BF16, F32 = jnp.bfloat16, jnp.float32
HIGHEST = lax.Precision.HIGHEST


def kernel(
    inc_hbm, hist_hbm, z_hbm, binv_hbm, pat_hbm, lc_ref, pat, wanted, cur_ref, fut_ref,
    inc, acc, zmat, binv, load, pass_out, pass_in, staged, staged_more, cut, slices, share_z, pat_in, pat0,
    base_out, base, share, share_out, share_in, *rest,
):
    mine, opposite, own, got = (rest[i * STEPS : (i + 1) * STEPS] for i in range(4))
    (
        local_sem, pass_ss, pass_rs, cut_ss, cut_rs, plane_ss, plane_rs, y_ss, y_rs, core_ss, core_rs,
        opp_ss, opp_rs, more_ss, more_rs, slice_ss, slice_rs, pat_ss, pat_rs, base_ss, base_rs, share_ss, share_rs,
    ) = rest[4 * STEPS :]
    d, q = lax.axis_index("delay"), lax.axis_index("row")
    y, k = d // 2, d % 2
    x, z = q // NZ, q % NZ
    rows = PIECES * 16
    other = y * 2 + 1 - k
    far = lax.rem(y + 2, NY) * 2 + k
    sent = []

    def remote(src, dst, ss, rs, dd, qq):
        return pltpu.make_async_remote_copy(
            src_ref=src, dst_ref=dst, send_sem=ss, recv_sem=rs, device_id=(dd, qq),
            device_id_type=pl.DeviceIdType.MESH,
        )

    def send(*args):
        copy = remote(*args)
        copy.start()
        sent.append((copy, None))

    def send_if(cond, *args):
        copy = remote(*args)
        pl.when(cond)(copy.start)
        sent.append((copy, cond))

    def arrived(dst, rs):
        remote(dst, dst, rs, rs, other, q).wait_recv()

    def left(src, ss):
        remote(src, src, ss, ss, other, q).wait_send()

    loads = [
        pltpu.make_async_copy(hist_hbm, acc, local_sem.at[0]),
        pltpu.make_async_copy(inc_hbm, inc, local_sem.at[1]),
        pltpu.make_async_copy(binv_hbm, binv, local_sem.at[2]),
        pltpu.make_async_copy(z_hbm, zmat, local_sem.at[3]),
    ]
    for start in loads:
        start.start()

    around = [lax.rem(d + s, PIECES) for s in range(1, PIECES)]
    plane = [
        lax.rem(x + a, NX) * NZ + lax.rem(z + s, NZ) for a in (0, 1, 3, 2) for s in (4, 3, 5, 2, 6, 1, 7, 0) if a or s
    ]
    barrier = pltpu.get_barrier_semaphore()
    peers = [(e, q) for e in around] + [(d, p) for p in plane]
    for peer in peers:
        pl.semaphore_signal(barrier, inc=1, device_id=peer, device_id_type=pl.DeviceIdType.MESH)

    def part_of(b):
        return pl.ds(b * rows if isinstance(b, int) else pl.multiple_of(b * rows, rows), rows)

    def invert(b, rhs):
        solved = jnp.dot(binv[b], rhs, precision=HIGHEST, preferred_element_type=F32)
        return solved.reshape(PIECES, 16, rows)

    def loaded(solved, coefficient):
        return (solved - coefficient * solved * solved * solved).astype(BF16)

    def slice_z(half):
        def body(i, carry):
            for s in range(PICKS):
                tile = zmat[half, part_of(i), pl.ds(s * rows, rows)]
                slices[half, :, i, s] = tile.T.reshape(PIECES, 16, rows)
            return carry

        lax.fori_loop(0, BLK, body, 0)

    for start in loads[:3]:
        start.wait()
    for i in range(BLK):
        load[i] = jnp.broadcast_to(lc_ref[pl.ds(i, 1), :], (rows, rows)).T.reshape(PIECES, 16, rows)

    @pl.when(d == 0)
    def _():
        for i in range(BLK):
            cut[:, i] = loaded(invert(i, inc[0, part_of(i), :].astype(F32) - acc[0, part_of(i), :]), load[i])
        mine[0][...] = cut[0]

    loads[3].wait()

    @pl.when(d == 0)
    def _():
        slice_z(0)
        share_z[0] = slices[0, 0]

    @pl.when(d < 2)
    def _():
        for i in range(BLK):
            base_out[:, i] = invert(i, inc[1 + d, part_of(i), :].astype(F32) - acc[1 - d, part_of(i), :])
        base[d] = base_out[d]

    pass_out[0] = acc[0].astype(BF16)

    @pl.when(d == PIECES - 1)
    def _():
        pass_in[...] = jnp.zeros_like(pass_in)

    pl.semaphore_wait(barrier, len(peers))

    def passing(n):
        return remote(pass_out.at[n], pass_in.at[n], pass_ss.at[n], pass_rs.at[n], lax.rem(d + PIECES - 1, PIECES), q)

    def pass_on(n):
        pl.when(d > 0)(passing(n).start)
        sent.append((passing(n), d > 0))

    def send_slices(half, which):
        for e in which:
            send_if(d == 0, slices.at[half, e], share_z.at[half], slice_ss.at[half, e], slice_rs.at[half], e, q)

    def product(n, half, i):
        total = None
        for s in range(0, PICKS, TOGETHER):
            picked = [got[n][:, pat[half, i, s + t]].reshape(rows, rows) for t in range(TOGETHER)]
            part = jnp.dot(
                zmat[half, part_of(i), pl.ds(s * rows, TOGETHER * rows)],
                jnp.concatenate(picked, axis=0),
                preferred_element_type=F32,
            )
            total = part if total is None else total + part
        return total

    def products(n, out):
        def first(i, carry):
            out[0, part_of(i), :] = acc[1, part_of(i), :] + product(n, 0, i)
            return carry

        lax.fori_loop(0, BLK, first, 0, unroll=True)
        if n < STEPS - 1:
            pass_out[n + 1] = out[0].astype(BF16)
            pass_on(n + 1)

        @pl.when(d < PIECES - 1)
        def _():
            arrived(pass_in.at[n], pass_rs.at[n])

        def second(i, carry):
            out[1, part_of(i), :] = pass_in[n, part_of(i), :].astype(F32) + product(n, 1, i)
            return carry

        lax.fori_loop(0, BLK, second, 0, unroll=True)
        cur_ref[n] = got[n][:, pl.ds(SLOTS, BLK)].transpose(1, 0, 2, 3)

    chunks = [(SLOTS, BLK)] + [(lax.rem(x + a, NX) * GROUP, GROUP) for a in (0, 3, 1, 2)]

    def spread(n, j):
        here = pl.ds(*chunks[j])
        for t, s in enumerate((1, 3)):
            remote(
                own[n].at[here], got[n].at[d, here], y_ss.at[n, t], y_rs.at[n, t], lax.rem(y + s, NY) * 2 + k, q
            ).start()

    def more(n):
        arrived(opposite[n], opp_rs.at[n])
        for t, p in enumerate(plane):
            for c in range(CAP):
                staged_more[n, t, c] = opposite[n][jnp.maximum(wanted[p, c, q], 0)]
            remote(
                staged_more.at[n, t], got[n].at[far, pl.ds(q * CAP, CAP)], more_ss.at[n], more_rs.at[n], d, p
            ).start()
        for c in range(CAP):
            got[n][far, q * CAP + c] = opposite[n][jnp.maximum(wanted[q, c, q], 0)]
        got[n][far, pl.ds(SLOTS, BLK)] = opposite[n][...]

    def across(n, e, t):
        src = own[n] if t == 3 else got[n].at[e]
        send(src, got[n].at[e], core_ss.at[n, t], core_rs.at[n, t], other, q)

    def hand_over(n):
        for t, s in enumerate((1, 3)):
            e = lax.rem(y + NY - s, NY) * 2 + k
            arrived(got[n].at[e], y_rs.at[n, t])
            across(n, e, t)
        arrived(got[n].at[far, pl.ds(0, SLOTS - CAP)], more_rs.at[n])
        across(n, far, 2)

    def gathered(n):
        for t, s in enumerate((1, 3, 2, 0)):
            arrived(got[n].at[lax.rem(y + NY - s, NY) * 2 + 1 - k], core_rs.at[n, t])

    for n in range(STEPS):
        if n == 0:
            for e in range(1, PIECES):
                send_if(d == 0, cut.at[e], mine[0], cut_ss.at[e], cut_rs.at[0], e, q)
            for e in range(1, PIECES):
                send_if(d == 0, pat_hbm, pat_in, pat_ss.at[e], pat_rs.at[0], e, q)
            send_slices(0, (4, 5, 2, 3, 6, 7, 1))

            @pl.when(d > 0)
            def _():
                arrived(mine[0], cut_rs.at[0])

        else:
            m = n - 1

            @pl.when(d != m)
            def _():
                arrived(base.at[m], base_rs.at[m])

            arrived(share_in.at[m, pl.ds(0, PIECES - 1)], share_rs.at[m])
            for i in range(BLK):
                solved = base[m, i] - share[i, d]
                for e in around:
                    solved = solved - share_in[m, e, i].astype(F32)
                mine[n][i] = loaded(solved, load[i, d])

        for t, p in enumerate(plane):
            for c in range(CAP):
                staged[n, t, c] = mine[n][jnp.maximum(wanted[p, c, q], 0)]
            remote(staged.at[n, t], own[n].at[pl.ds(q * CAP, CAP)], plane_ss.at[n], plane_rs.at[n, x], d, p).start()
        for c in range(CAP):
            own[n][q * CAP + c] = mine[n][jnp.maximum(wanted[q, c, q], 0)]
        own[n][pl.ds(SLOTS, BLK)] = mine[n][...]
        send(mine[n], opposite[n], opp_ss.at[n], opp_rs.at[n], far, q)

        if n == 0:
            for m in range(2):
                for s, e in enumerate(around):
                    send_if(d == m, base_out.at[e], base.at[m], base_ss.at[m, s], base_rs.at[m], e, q)
            pass_on(0)

            @pl.when(d == 0)
            def _():
                slice_z(1)
                share_z[1] = slices[1, 0]

            send_slices(1, EARLY)

            @pl.when(d > 0)
            def _():
                arrived(pat_in, pat_rs.at[0])

            @pl.when(d == 0)
            def _():
                copy = pltpu.make_async_copy(pat_hbm, pat_in, local_sem.at[4])
                copy.start()
                copy.wait()

            copy = pltpu.make_async_copy(pat_in, pat0, local_sem.at[5])
            copy.start()
            copy.wait()
        if n == 1:
            for j in range(len(chunks)):
                spread(n - 1, j)
        if n == STEPS - 1:
            gathered(n - 2)
            products(n - 2, acc)
            more(n)
            spread(n, 0)

        for j, a in enumerate((0, 3, 1, 2), 1):
            from_x = lax.rem(x + a, NX)
            there = pl.ds(0, GROUP - CAP) if a == 0 else pl.ds(*chunks[j])
            arrived(own[n].at[there], plane_rs.at[n, from_x])
            if n == STEPS - 1:
                spread(n, j)
                if j == len(chunks) - 1:
                    hand_over(n - 1)
        got[n][d] = own[n][...]

        if n < STEPS - 1:
            @pl.when(d > 0)
            def _():
                arrived(share_z.at[n], slice_rs.at[n])

            def body(i, carry):
                total = None
                for half in range(n + 1):
                    picked = jnp.concatenate([own[n - half][pat0[half, i, s]] for s in range(PICKS)], axis=0)
                    part = lax.dot_general(
                        share_z[half, i].reshape(PICKS * 16, rows), picked, (((0,), (0,)), ((), ())),
                        preferred_element_type=F32,
                    )
                    total = part if total is None else total + part
                solved = invert(i, total)
                share[i] = solved
                share_out[n, :, i] = solved.astype(BF16)
                return carry

            lax.fori_loop(0, BLK, body, 0)
            for s, e in enumerate(around):
                send(share_out.at[n, e], share_in.at[n, d], share_ss.at[n, s], share_rs.at[n], e, q)
            if n == 0:
                send_slices(1, [e for e in (4, 5, 3, 7) if e not in EARLY])
            if n == 1:
                for j in range(len(chunks)):
                    spread(n, j)
            more(n)
        across(n, d, 3)
        if n == 1:
            hand_over(n - 1)

    gathered(n - 1)
    products(n - 1, acc)
    hand_over(n)
    gathered(n)
    products(n, fut_ref)
    for n in range(STEPS):
        left(staged.at[n], plane_ss.at[n])
        left(staged_more.at[n], more_ss.at[n])
        for t in range(2):
            left(own[n], y_ss.at[n, t])
    for copy, cond in sent:
        if cond is None:
            copy.wait_send()
        else:
            pl.when(cond)(copy.wait_send)


def local(incident, history, couplings, block_inverse, load_coeff, pattern, wanted):
    size = block_inverse.shape[1]
    rows = BLK * size
    anywhere = pl.BlockSpec(memory_space=pl.ANY)
    numbers = pl.BlockSpec(memory_space=pltpu.SMEM)
    vmem = pl.BlockSpec(memory_space=pltpu.VMEM)
    dma = pltpu.SemaphoreType.DMA
    currents, future = pl.pallas_call(
        kernel,
        out_shape=(
            pltpu.VMEM((STEPS, BLK, PIECES, 16, size), BF16),
            pltpu.VMEM((2, rows, size), F32),
        ),
        in_specs=[anywhere] * 5 + [vmem, numbers, numbers],
        out_specs=(vmem, vmem),
        scratch_shapes=[
            pltpu.VMEM((STEPS, rows, size), BF16),
            pltpu.VMEM((2, rows, size), F32),
            pltpu.VMEM((2, rows, PICKS * size), BF16),
            pltpu.VMEM((BLK, size, size), F32),
            pltpu.VMEM((BLK, PIECES, 16, size), F32),
            pltpu.VMEM((STEPS, rows, size), BF16),
            pltpu.VMEM((STEPS, rows, size), BF16),
            pltpu.VMEM((STEPS, OWNERS - 1, CAP, 16, size), BF16),
            pltpu.VMEM((STEPS, OWNERS - 1, CAP, 16, size), BF16),
            pltpu.VMEM((PIECES, BLK, 16, size), BF16),
            pltpu.VMEM((2, PIECES, BLK, PICKS, 16, size), BF16),
            pltpu.VMEM((2, BLK, PICKS, 16, size), BF16),
            pltpu.VMEM(pattern.shape, jnp.int32),
            pltpu.SMEM(pattern.shape, jnp.int32),
            pltpu.VMEM((PIECES, BLK, 16, size), F32),
            pltpu.VMEM((STEPS - 1, BLK, 16, size), F32),
            pltpu.VMEM((BLK, PIECES, 16, size), F32),
            pltpu.VMEM((STEPS - 1, PIECES, BLK, 16, size), BF16),
            pltpu.VMEM((STEPS - 1, PIECES, BLK, 16, size), BF16),
            *[pltpu.VMEM((BLK, 16, size), BF16) for _ in range(2 * STEPS)],
            *[pltpu.VMEM((SLOTS + BLK, 16, size), BF16) for _ in range(STEPS)],
            *[pltpu.VMEM((PIECES, SLOTS + BLK, 16, size), BF16) for _ in range(STEPS)],
            dma((6,)),
            dma((STEPS,)), dma((STEPS,)),
            dma((PIECES,)), dma((1,)),
            dma((STEPS,)), dma((STEPS, NX)),
            dma((STEPS, 2)), dma((STEPS, 2)),
            dma((STEPS, NY)), dma((STEPS, NY)),
            dma((STEPS,)), dma((STEPS,)),
            dma((STEPS,)), dma((STEPS,)),
            dma((2, PIECES)), dma((2,)),
            dma((PIECES,)), dma((1,)),
            dma((2, PIECES)), dma((2,)),
            dma((STEPS - 1, PIECES)), dma((STEPS - 1,)),
        ],
        compiler_params=pltpu.CompilerParams(
            collective_id=0, has_side_effects=True, vmem_limit_bytes=60 * 2**20
        ),
        name="march",
    )(
        incident, history, couplings, block_inverse, pattern, load_coeff.reshape(BLK, size),
        pattern, wanted.transpose(0, 2, 1),
    )
    return currents.reshape(STEPS, rows, size), future


def solution(mesh):
    in_specs = (
        P(None, "row", None),
        P("delay", "row", None),
        P("delay", "row", None),
        P("row", None, None),
        P("row"),
        P("delay", "row", None),
        P(),
    )
    out_specs = (P(None, "row", None), P("delay", "row", None))
    return jax.shard_map(local, mesh=mesh, in_specs=in_specs, out_specs=out_specs, check_vma=False)
```

```python
import jax
import jax.numpy as jnp
from jax import lax
from jax.experimental import pallas as pl
from jax.experimental.pallas import tpu as pltpu
from jax.sharding import PartitionSpec as P

STEPS = 3
NX, NY, NZ = 4, 4, 8
OWNERS = NX * NZ
PIECES = 2 * NY
BLK = 4
CAP = 2
GROUP = NZ * CAP
SLOTS = NX * GROUP
PICKS = 16
TOGETHER = 16
EARLY = (1, 2, 6)
BF16, F32 = jnp.bfloat16, jnp.float32
HIGHEST = lax.Precision.HIGHEST


def kernel(
    inc_hbm, hist_hbm, z_hbm, binv_hbm, pat_hbm, lc_ref, pat, wanted, cur_ref, fut_ref,
    inc, acc, zmat, binv, load, pass_out, pass_in, staged, staged_more, cut, slices, share_z, pat_in, pat0,
    base_out, base, share, share_out, share_in, *rest,
):
    mine, opposite, own, got = (rest[i * STEPS : (i + 1) * STEPS] for i in range(4))
    (
        local_sem, pass_ss, pass_rs, cut_ss, cut_rs, plane_ss, plane_rs, y_ss, y_rs, core_ss, core_rs,
        opp_ss, opp_rs, more_ss, more_rs, slice_ss, slice_rs, pat_ss, pat_rs, base_ss, base_rs, share_ss, share_rs,
    ) = rest[4 * STEPS :]
    d, q = lax.axis_index("delay"), lax.axis_index("row")
    y, k = d // 2, d % 2
    x, z = q // NZ, q % NZ
    rows = PIECES * 16
    other = y * 2 + 1 - k
    far = lax.rem(y + 2, NY) * 2 + k
    sent = []

    def remote(src, dst, ss, rs, dd, qq):
        return pltpu.make_async_remote_copy(
            src_ref=src, dst_ref=dst, send_sem=ss, recv_sem=rs, device_id=(dd, qq),
            device_id_type=pl.DeviceIdType.MESH,
        )

    def send(*args):
        copy = remote(*args)
        copy.start()
        sent.append((copy, None))

    def send_if(cond, *args):
        copy = remote(*args)
        pl.when(cond)(copy.start)
        sent.append((copy, cond))

    def arrived(dst, rs):
        remote(dst, dst, rs, rs, other, q).wait_recv()

    def left(src, ss):
        remote(src, src, ss, ss, other, q).wait_send()

    loads = [
        pltpu.make_async_copy(hist_hbm, acc, local_sem.at[0]),
        pltpu.make_async_copy(inc_hbm, inc, local_sem.at[1]),
        pltpu.make_async_copy(binv_hbm, binv, local_sem.at[2]),
        pltpu.make_async_copy(z_hbm, zmat, local_sem.at[3]),
    ]
    for start in loads:
        start.start()

    around = [lax.rem(d + s, PIECES) for s in (4, 3, 5, 2, 6, 7, 1)]
    plane = [
        lax.rem(x + a, NX) * NZ + lax.rem(z + s, NZ) for a in (0, 1, 3, 2) for s in (4, 3, 5, 2, 6, 1, 7, 0) if a or s
    ]
    barrier = pltpu.get_barrier_semaphore()
    peers = [(e, q) for e in around] + [(d, p) for p in plane]
    for peer in peers:
        pl.semaphore_signal(barrier, inc=1, device_id=peer, device_id_type=pl.DeviceIdType.MESH)

    def part_of(b):
        return pl.ds(b * rows if isinstance(b, int) else pl.multiple_of(b * rows, rows), rows)

    def invert(b, rhs):
        solved = jnp.dot(binv[b], rhs, precision=HIGHEST, preferred_element_type=F32)
        return solved.reshape(PIECES, 16, rows)

    def loaded(solved, coefficient):
        return (solved - coefficient * solved * solved * solved).astype(BF16)

    def slice_z(half):
        def body(i, carry):
            for s in range(PICKS):
                tile = zmat[half, part_of(i), pl.ds(s * rows, rows)]
                slices[half, :, i, s] = tile.T.reshape(PIECES, 16, rows)
            return carry

        lax.fori_loop(0, BLK, body, 0)

    for start in loads[:3]:
        start.wait()
    for i in range(BLK):
        load[i] = jnp.broadcast_to(lc_ref[pl.ds(i, 1), :], (rows, rows)).T.reshape(PIECES, 16, rows)

    @pl.when(d == 0)
    def _():
        for i in range(BLK):
            cut[:, i] = loaded(invert(i, inc[0, part_of(i), :].astype(F32) - acc[0, part_of(i), :]), load[i])
        mine[0][...] = cut[0]

    loads[3].wait()

    @pl.when(d == 0)
    def _():
        slice_z(0)
        share_z[0] = slices[0, 0]

    @pl.when(d < 2)
    def _():
        for i in range(BLK):
            base_out[:, i] = invert(i, inc[1 + d, part_of(i), :].astype(F32) - acc[1 - d, part_of(i), :])
        base[d] = base_out[d]

    pass_out[0] = acc[0].astype(BF16)

    @pl.when(d == PIECES - 1)
    def _():
        pass_in[...] = jnp.zeros_like(pass_in)

    pl.semaphore_wait(barrier, len(peers))

    def passing(n):
        return remote(pass_out.at[n], pass_in.at[n], pass_ss.at[n], pass_rs.at[n], lax.rem(d + PIECES - 1, PIECES), q)

    def pass_on(n):
        pl.when(d > 0)(passing(n).start)
        sent.append((passing(n), d > 0))

    def send_slices(half, which):
        for e in which:
            send_if(d == 0, slices.at[half, e], share_z.at[half], slice_ss.at[half, e], slice_rs.at[half], e, q)

    def product(n, half, i):
        total = None
        for s in range(0, PICKS, TOGETHER):
            picked = [got[n][:, pat[half, i, s + t]].reshape(rows, rows) for t in range(TOGETHER)]
            part = jnp.dot(
                zmat[half, part_of(i), pl.ds(s * rows, TOGETHER * rows)],
                jnp.concatenate(picked, axis=0),
                preferred_element_type=F32,
            )
            total = part if total is None else total + part
        return total

    def products(n, out):
        def first(i, carry):
            out[0, part_of(i), :] = acc[1, part_of(i), :] + product(n, 0, i)
            return carry

        lax.fori_loop(0, BLK, first, 0, unroll=True)
        if n < STEPS - 1:
            pass_out[n + 1] = out[0].astype(BF16)
            pass_on(n + 1)

        @pl.when(d < PIECES - 1)
        def _():
            arrived(pass_in.at[n], pass_rs.at[n])

        def second(i, carry):
            out[1, part_of(i), :] = pass_in[n, part_of(i), :].astype(F32) + product(n, 1, i)
            return carry

        lax.fori_loop(0, BLK, second, 0, unroll=True)
        cur_ref[n] = got[n][:, pl.ds(SLOTS, BLK)].transpose(1, 0, 2, 3)

    chunks = [(SLOTS, BLK)] + [(lax.rem(x + a, NX) * GROUP, GROUP) for a in (0, 3, 1, 2)]

    def spread(n, j):
        here = pl.ds(*chunks[j])
        for t, s in enumerate((1, 3)):
            remote(
                own[n].at[here], got[n].at[d, here], y_ss.at[n, t], y_rs.at[n, t], lax.rem(y + s, NY) * 2 + k, q
            ).start()

    def more(n):
        arrived(opposite[n], opp_rs.at[n])
        for t, p in enumerate(plane):
            for c in range(CAP):
                staged_more[n, t, c] = opposite[n][jnp.maximum(wanted[p, c, q], 0)]
            remote(
                staged_more.at[n, t], got[n].at[far, pl.ds(q * CAP, CAP)], more_ss.at[n], more_rs.at[n], d, p
            ).start()
        for c in range(CAP):
            got[n][far, q * CAP + c] = opposite[n][jnp.maximum(wanted[q, c, q], 0)]
        got[n][far, pl.ds(SLOTS, BLK)] = opposite[n][...]

    def across(n, e, t):
        src = own[n] if t == 3 else got[n].at[e]
        send(src, got[n].at[e], core_ss.at[n, t], core_rs.at[n, t], other, q)

    def hand_over(n):
        for t, s in enumerate((1, 3)):
            e = lax.rem(y + NY - s, NY) * 2 + k
            arrived(got[n].at[e], y_rs.at[n, t])
            across(n, e, t)
        arrived(got[n].at[far, pl.ds(0, SLOTS - CAP)], more_rs.at[n])
        across(n, far, 2)

    def gathered(n):
        for t, s in enumerate((1, 3, 2, 0)):
            arrived(got[n].at[lax.rem(y + NY - s, NY) * 2 + 1 - k], core_rs.at[n, t])

    for n in range(STEPS):
        if n == 0:
            for e in (4, 5, 2, 3, 6, 7, 1):
                send_if(d == 0, cut.at[e], mine[0], cut_ss.at[e], cut_rs.at[0], e, q)
            for e in range(1, PIECES):
                send_if(d == 0, pat_hbm, pat_in, pat_ss.at[e], pat_rs.at[0], e, q)
            send_slices(0, (4, 5, 2, 3, 6, 7, 1))

            @pl.when(d > 0)
            def _():
                arrived(mine[0], cut_rs.at[0])

        else:
            m = n - 1

            @pl.when(d != m)
            def _():
                arrived(base.at[m], base_rs.at[m])

            arrived(share_in.at[m, pl.ds(0, PIECES - 1)], share_rs.at[m])
            for i in range(BLK):
                solved = base[m, i] - share[i, d]
                for e in around:
                    solved = solved - share_in[m, e, i].astype(F32)
                mine[n][i] = loaded(solved, load[i, d])

        for t, p in enumerate(plane):
            for c in range(CAP):
                staged[n, t, c] = mine[n][jnp.maximum(wanted[p, c, q], 0)]
            remote(staged.at[n, t], own[n].at[pl.ds(q * CAP, CAP)], plane_ss.at[n], plane_rs.at[n, x], d, p).start()
        for c in range(CAP):
            own[n][q * CAP + c] = mine[n][jnp.maximum(wanted[q, c, q], 0)]
        own[n][pl.ds(SLOTS, BLK)] = mine[n][...]
        send(mine[n], opposite[n], opp_ss.at[n], opp_rs.at[n], far, q)

        if n == 0:
            for m in range(2):
                for s, e in enumerate(around):
                    send_if(d == m, base_out.at[e], base.at[m], base_ss.at[m, s], base_rs.at[m], e, q)
            pass_on(0)

            @pl.when(d == 0)
            def _():
                slice_z(1)
                share_z[1] = slices[1, 0]

            send_slices(1, EARLY)

            @pl.when(d > 0)
            def _():
                arrived(pat_in, pat_rs.at[0])

            @pl.when(d == 0)
            def _():
                copy = pltpu.make_async_copy(pat_hbm, pat_in, local_sem.at[4])
                copy.start()
                copy.wait()

            copy = pltpu.make_async_copy(pat_in, pat0, local_sem.at[5])
            copy.start()
            copy.wait()
        if n == 1:
            for j in range(len(chunks)):
                spread(n - 1, j)
        if n == STEPS - 1:
            gathered(n - 2)
            products(n - 2, acc)
            more(n)
            spread(n, 0)

        for j, a in enumerate((0, 3, 1, 2), 1):
            from_x = lax.rem(x + a, NX)
            there = pl.ds(0, GROUP - CAP) if a == 0 else pl.ds(*chunks[j])
            arrived(own[n].at[there], plane_rs.at[n, from_x])
            if n == STEPS - 1:
                spread(n, j)
                if j == len(chunks) - 1:
                    hand_over(n - 1)
        got[n][d] = own[n][...]

        if n < STEPS - 1:
            @pl.when(d > 0)
            def _():
                arrived(share_z.at[n], slice_rs.at[n])

            def body(i, carry):
                total = None
                for half in range(n + 1):
                    picked = jnp.concatenate([own[n - half][pat0[half, i, s]] for s in range(PICKS)], axis=0)
                    part = lax.dot_general(
                        share_z[half, i].reshape(PICKS * 16, rows), picked, (((0,), (0,)), ((), ())),
                        preferred_element_type=F32,
                    )
                    total = part if total is None else total + part
                solved = invert(i, total)
                share[i] = solved
                share_out[n, :, i] = solved.astype(BF16)
                return carry

            lax.fori_loop(0, BLK, body, 0)
            for s, e in enumerate(around):
                send(share_out.at[n, e], share_in.at[n, d], share_ss.at[n, s], share_rs.at[n], e, q)
            if n == 0:
                send_slices(1, [e for e in (4, 5, 3, 7) if e not in EARLY])
            if n == 1:
                for j in range(len(chunks)):
                    spread(n, j)
            more(n)
        across(n, d, 3)
        if n == 1:
            hand_over(n - 1)

    gathered(n - 1)
    products(n - 1, acc)
    hand_over(n)
    gathered(n)
    products(n, fut_ref)
    for n in range(STEPS):
        left(staged.at[n], plane_ss.at[n])
        left(staged_more.at[n], more_ss.at[n])
        for t in range(2):
            left(own[n], y_ss.at[n, t])
    for copy, cond in sent:
        if cond is None:
            copy.wait_send()
        else:
            pl.when(cond)(copy.wait_send)


def local(incident, history, couplings, block_inverse, load_coeff, pattern, wanted):
    size = block_inverse.shape[1]
    rows = BLK * size
    anywhere = pl.BlockSpec(memory_space=pl.ANY)
    numbers = pl.BlockSpec(memory_space=pltpu.SMEM)
    vmem = pl.BlockSpec(memory_space=pltpu.VMEM)
    dma = pltpu.SemaphoreType.DMA
    currents, future = pl.pallas_call(
        kernel,
        out_shape=(
            pltpu.VMEM((STEPS, BLK, PIECES, 16, size), BF16),
            pltpu.VMEM((2, rows, size), F32),
        ),
        in_specs=[anywhere] * 5 + [vmem, numbers, numbers],
        out_specs=(vmem, vmem),
        scratch_shapes=[
            pltpu.VMEM((STEPS, rows, size), BF16),
            pltpu.VMEM((2, rows, size), F32),
            pltpu.VMEM((2, rows, PICKS * size), BF16),
            pltpu.VMEM((BLK, size, size), F32),
            pltpu.VMEM((BLK, PIECES, 16, size), F32),
            pltpu.VMEM((STEPS, rows, size), BF16),
            pltpu.VMEM((STEPS, rows, size), BF16),
            pltpu.VMEM((STEPS, OWNERS - 1, CAP, 16, size), BF16),
            pltpu.VMEM((STEPS, OWNERS - 1, CAP, 16, size), BF16),
            pltpu.VMEM((PIECES, BLK, 16, size), BF16),
            pltpu.VMEM((2, PIECES, BLK, PICKS, 16, size), BF16),
            pltpu.VMEM((2, BLK, PICKS, 16, size), BF16),
            pltpu.VMEM(pattern.shape, jnp.int32),
            pltpu.SMEM(pattern.shape, jnp.int32),
            pltpu.VMEM((PIECES, BLK, 16, size), F32),
            pltpu.VMEM((STEPS - 1, BLK, 16, size), F32),
            pltpu.VMEM((BLK, PIECES, 16, size), F32),
            pltpu.VMEM((STEPS - 1, PIECES, BLK, 16, size), BF16),
            pltpu.VMEM((STEPS - 1, PIECES, BLK, 16, size), BF16),
            *[pltpu.VMEM((BLK, 16, size), BF16) for _ in range(2 * STEPS)],
            *[pltpu.VMEM((SLOTS + BLK, 16, size), BF16) for _ in range(STEPS)],
            *[pltpu.VMEM((PIECES, SLOTS + BLK, 16, size), BF16) for _ in range(STEPS)],
            dma((6,)),
            dma((STEPS,)), dma((STEPS,)),
            dma((PIECES,)), dma((1,)),
            dma((STEPS,)), dma((STEPS, NX)),
            dma((STEPS, 2)), dma((STEPS, 2)),
            dma((STEPS, NY)), dma((STEPS, NY)),
            dma((STEPS,)), dma((STEPS,)),
            dma((STEPS,)), dma((STEPS,)),
            dma((2, PIECES)), dma((2,)),
            dma((PIECES,)), dma((1,)),
            dma((2, PIECES)), dma((2,)),
            dma((STEPS - 1, PIECES)), dma((STEPS - 1,)),
        ],
        compiler_params=pltpu.CompilerParams(
            collective_id=0, has_side_effects=True, vmem_limit_bytes=60 * 2**20
        ),
        name="march",
    )(
        incident, history, couplings, block_inverse, pattern, load_coeff.reshape(BLK, size),
        pattern, wanted.transpose(0, 2, 1),
    )
    return currents.reshape(STEPS, rows, size), future


def solution(mesh):
    in_specs = (
        P(None, "row", None),
        P("delay", "row", None),
        P("delay", "row", None),
        P("row", None, None),
        P("row"),
        P("delay", "row", None),
        P(),
    )
    out_specs = (P(None, "row", None), P("delay", "row", None))
    return jax.shard_map(local, mesh=mesh, in_specs=in_specs, out_specs=out_specs, check_vma=False)
```
